256 devices in a mesh: sec: 2 (over y_lo), dp: 16 (over x, y_hi, core), tp: 8 (over z).
Axes of the slice: x: 4, y: 4 (y_hi: 2, y_lo: 2; y = y_hi * 2 + y_lo), z: 8, core: 2. Of those that a mesh axis runs over, the one named last changes fastest.
Arguments:
- patches: bfloat16 [32, 448, 1176], P(('sec', 'dp'), 'tp'), may hold values from -6 to 6
- counts: int32 [32], replicated, may hold values from 16 to 112, as said below
- positions: int32 [32, 112], P(('sec', 'dp')), may hold values from 0 to 127, as said below
- pe_weight: bfloat16 [1176, 1280], P(None, ('sec', 'dp')), may hold values from -0.1875 to 0.1875
- ln_gain: float32 [1280], replicated, may hold values from 0.5 to 1.5
- ln_bias: float32 [1280], replicated, may hold values from -1.5 to 1.5
- w_in: bfloat16 [5120, 2560], P(None, 'tp'), may hold values from -0.078125 to 0.078125
- b_in: float32 [2560], P('tp'), may hold values from -2.5 to 2.5
- w_out: bfloat16 [2560, 8192], P('tp'), may hold values from -0.125 to 0.125
- b_out: float32 [8192], P('tp'), may hold values from -2.5 to 2.5
- text_embeds: bfloat16 [32, 128, 8192], P(('sec', 'dp'), None, 'tp'), may hold values from -6 to 6
- rms_gain: float32 [8192], P('tp'), may hold values from 0.5 to 1.5
- kv_weight: bfloat16 [8192, 2048], P(('sec', 'dp'), 'tp'), may hold values from -0.0625 to 0.0625
- kv_cotangent: bfloat16 [32, 128, 2048], P(('sec', 'dp'), None, 'tp'), may hold values from -6 to 6
Outputs:
- keys_values: bfloat16 [32, 128, 2048], P(('sec', 'dp'), None, 'tp')
- sequence_grad: bfloat16 [32, 128, 8192], P(('sec', 'dp'), None, 'tp')
- vision_grad: bfloat16 [32, 112, 8192], P(('sec', 'dp'), None, 'tp')
- kv_weight_grad: float32 [8192, 2048], P(('sec', 'dp'), 'tp')
The draws below stay inside these ranges and needn't reach their ends.
Inputs may be any that keep to these rules, and one draw needn't show every extreme that they name: Samples pair up within each half: for every i whose remainder modulo 32/2 is below 8, counts[i] + counts[i + 8] = 128. `positions`: the 112 entries of a row are distinct.
All inputs are finite; a program needn't handle non-finite values.
Results may differ from the reference program's by a relative error of at most 0.007.
Values may be sent and summed in bfloat16 or wider, within the bound.
No kernel may reach another device: no remote copies, remote signals or barrier semaphores. Data moves between devices by JAX's collectives and lax.ppermute only.
A program may use at most 64 MiB of HBM per device.

```python
import jax
import jax.numpy as jnp
from jax import lax

WIDTH = 8192
VIS_WIDTH = 1280
PATCH_VALUES = 1176
MERGE_PATCHES = 4
KV_COLUMNS = 2048
MERGER_HIDDEN = 2560
MEAN_TOKENS = 64
TEXT_LEN = 128
EXTRA_TOKENS = 48
MOST_TOKENS = 112
SAMPLES = 32
N_DP = 16


def draw_counts(key, part):
    key = jax.random.fold_in(key, 11)
    half_pairs = N_DP // 2
    key_extra, key_side, key_pick = jax.random.split(key, 3)
    extra = jax.random.randint(key_extra, (2, half_pairs), EXTRA_TOKENS // 3, EXTRA_TOKENS + 1)
    chosen = jax.random.randint(key_pick, (2, 1), 0, half_pairs)
    extra = jnp.where(jnp.arange(half_pairs)[None, :] == chosen, EXTRA_TOKENS, extra)
    heavy_side = jax.random.randint(key_side, (2, half_pairs), 0, 2) * 2 - 1
    heavy = MEAN_TOKENS + heavy_side * extra
    light = MEAN_TOKENS - heavy_side * extra
    return jnp.concatenate([heavy, light], axis=1).reshape(2 * N_DP).astype(jnp.int32)


def draw_positions(key, part):
    key = jax.random.fold_in(key, 23)
    row_keys = jax.random.split(key, 2 * N_DP)

    def one_row(row_key):
        key_fill, key_order = jax.random.split(row_key)
        inner = jax.random.permutation(key_fill, TEXT_LEN - 2)[:MOST_TOKENS - 2].astype(jnp.int32) + 1
        chosen = jnp.concatenate([jnp.array([0, TEXT_LEN - 1], dtype=jnp.int32), inner])
        return chosen[jax.random.permutation(key_order, MOST_TOKENS)]
    return jax.vmap(one_row)(row_keys).astype(jnp.int32)


def strengthened(entries, stream_key, source, target, shards_of, factor):
    owner, partner = [(jnp.arange(entries.shape[position]) // (entries.shape[position] // shards_of)).reshape([-1 if axis == position else 1 for axis in range(entries.ndim)]) for position in (source, target)]
    chosen = jax.random.permutation(stream_key, shards_of)[partner]
    strong = (owner == chosen) | (owner == (partner + shards_of // 2) % shards_of)
    return jnp.where(strong, factor * entries, entries)


def level_of(rng, extent, shards, low, top_value):
    factor_of = 1.0
    for position, shards_of in shards:
        steps = jax.random.uniform(jax.random.fold_in(jax.random.fold_in(rng, 6), position), (shards_of,), jnp.float32, low / len(shards), top_value / len(shards))
        factor_of = factor_of * jnp.repeat(jnp.exp(steps), extent[position] // shards_of).reshape((-1,) + (1,) * (len(extent) - 1 - position))
    return factor_of


def centred(own_key, shape, deviation, limit, cuts=(), kind=jnp.bfloat16):
    values = deviation * jax.random.normal(own_key, shape, jnp.float32)
    if cuts:
        values = values * level_of(own_key, shape, cuts, -0.22, 0.18)
    return jnp.clip(values, -limit, limit).astype(kind)


def noise_with(stream_key, dims, spread, reach, cuts, heavy, kind=jnp.bfloat16):
    values = spread * jax.random.normal(stream_key, dims, jnp.float32)
    if cuts:
        values = values * level_of(stream_key, dims, cuts, -0.22, 0.18)
    return jnp.clip(strengthened(values, jax.random.fold_in(stream_key, 3), *heavy), -reach, reach).astype(kind)


def setup_inputs(seed: int = 0) -> dict:
    key_list = jax.random.split(jax.random.key(seed), 15)
    return {
        "patches": centred(key_list[0], (SAMPLES, MERGE_PATCHES * MOST_TOKENS, PATCH_VALUES), 1.0, 6.0, ((0, 32), (1, 8))),
        "counts": draw_counts(jax.random.fold_in(key_list[14], 71), 0),
        "positions": draw_positions(jax.random.fold_in(key_list[14], 71), 0),
        "pe_weight": centred(key_list[3], (PATCH_VALUES, VIS_WIDTH), PATCH_VALUES ** -0.5, 0.1875, ((1, 32),)),
        "ln_gain": jnp.clip(1.0 + 0.1 * jax.random.normal(key_list[4], (VIS_WIDTH,), jnp.float32), 0.5, 1.5),
        "ln_bias": centred(key_list[5], (VIS_WIDTH,), 0.3, 1.5, (), jnp.float32),
        "w_in": centred(key_list[6], (MERGE_PATCHES * VIS_WIDTH, MERGER_HIDDEN), (MERGE_PATCHES * VIS_WIDTH) ** -0.5, 0.078125, ((1, 8),)),
        "b_in": centred(key_list[7], (MERGER_HIDDEN,), 0.5, 2.5, ((0, 8),), jnp.float32),
        "w_out": centred(key_list[8], (MERGER_HIDDEN, WIDTH), MERGER_HIDDEN ** -0.5, 0.125, ((0, 8),)),
        "b_out": centred(key_list[9], (WIDTH,), 0.5, 2.5, ((0, 8),), jnp.float32),
        "text_embeds": noise_with(key_list[10], (SAMPLES, TEXT_LEN, WIDTH), 1.0, 6.0, ((0, 32), (2, 8)), (0, 2, 32, 2.75)),
        "rms_gain": jnp.clip(1.0 + 0.1 * jax.random.normal(key_list[11], (WIDTH,), jnp.float32), 0.5, 1.5),
        "kv_weight": centred(key_list[12], (WIDTH, KV_COLUMNS), WIDTH ** -0.5, 0.0625, ((0, 32), (1, 8))),
        "kv_cotangent": centred(key_list[13], (SAMPLES, TEXT_LEN, KV_COLUMNS), 1.0, 6.0, ((0, 32), (2, 8))),
    }


def layer_norm(values, gain_vector, bias_vector):
    average = lax.optimization_barrier(jnp.mean(values, axis=-1, keepdims=True))
    centered = values - average
    variance = lax.optimization_barrier(jnp.mean(centered * centered, axis=-1, keepdims=True))
    return centered * lax.rsqrt(variance + 1e-06) * gain_vector + bias_vector

def reference(patches, counts, positions, pe_weight, ln_gain, ln_bias, w_in, b_in, w_out, b_out, text_embeds, rms_gain, kv_weight, kv_cotangent):

    def encode(sample_patches):
        projected = jnp.dot(sample_patches, pe_weight, preferred_element_type=jnp.float32)
        embedded = layer_norm(projected, ln_gain, ln_bias).astype(jnp.bfloat16)
        merged = embedded.reshape(MOST_TOKENS, MERGE_PATCHES * VIS_WIDTH)
        before_gelu = jnp.dot(merged, w_in, preferred_element_type=jnp.float32) + b_in
        hidden = jax.nn.gelu(before_gelu, approximate=False).astype(jnp.bfloat16)
        return (jnp.dot(hidden, w_out, preferred_element_type=jnp.float32) + b_out).astype(jnp.bfloat16)
    vision = lax.map(encode, patches)
    vision_seq = jnp.roll(vision, -N_DP, axis=0)
    count_seq = jnp.roll(counts, -N_DP, axis=0)

    def forward(inputs):
        text_rows, vision_rows, slot_positions, image_count, cotangent = inputs
        slot_index = jnp.arange(MOST_TOKENS, dtype=jnp.int32)
        line_index = jnp.arange(TEXT_LEN, dtype=jnp.int32)
        selector = (slot_positions[None, :] == line_index[:, None]) & (slot_index[None, :] < image_count)
        selector = selector.astype(jnp.float32)
        placed = jnp.dot(selector, vision_rows.astype(jnp.float32), precision=lax.Precision.HIGHEST)
        image_rows = lax.optimization_barrier(jnp.sum(selector, axis=1, keepdims=True)) > 0.5
        combined = jnp.where(image_rows, placed, text_rows.astype(jnp.float32))
        row_scale = lax.rsqrt(lax.optimization_barrier(jnp.mean(combined * combined, axis=1, keepdims=True)) + 1e-06)
        normed = (combined * row_scale * rms_gain).astype(jnp.bfloat16)
        keys_out = jnp.dot(normed, kv_weight, preferred_element_type=jnp.float32).astype(jnp.bfloat16)
        normed_grad = jnp.dot(cotangent, kv_weight.T, preferred_element_type=jnp.float32)
        scaled = normed_grad * rms_gain
        row_dot = lax.optimization_barrier(jnp.sum(scaled * combined, axis=1, keepdims=True))
        seq_grad = (row_scale * scaled - combined * row_scale * row_scale * row_scale * row_dot / WIDTH).astype(jnp.bfloat16)
        image_grad = jnp.dot(selector.T, seq_grad.astype(jnp.float32), precision=lax.Precision.HIGHEST).astype(jnp.bfloat16)
        return (keys_out, seq_grad, image_grad, normed)
    keys_values, sequence_grad, image_grad, normed = lax.map(forward, (text_embeds, vision_seq, positions, count_seq, kv_cotangent))
    vision_grad = jnp.roll(image_grad, N_DP, axis=0)
    kv_weight_grad = jnp.dot(normed.reshape(-1, WIDTH).T, kv_cotangent.reshape(-1, KV_COLUMNS), preferred_element_type=jnp.float32)
    return (keys_values, sequence_grad, vision_grad, kv_weight_grad)
```

```python
import jax
import jax.numpy as jnp
from jax import lax
from jax.experimental import pallas as pl
from jax.sharding import PartitionSpec as P

WIDTH = 8192
MERGE_PATCHES = 4
PLANE = ("sec", "dp")
ALL = ("sec", "dp", "tp")
N_TP = 8
BF = jnp.bfloat16
F32 = jnp.float32


def plane_index(x, y, core):
    return (y % 2) * 16 + x * 4 + (y // 2) * 2 + core


SAME_CORE = [
    [plane_index(x, y, core) for lo in range(2) for x in range(4) for y in (lo, lo + 2)]
    for core in range(2)
]
SAME_X = [[plane_index(x, y, core) for y in range(4)] for x in range(4) for core in range(2)]
SAME_Y = [[plane_index(x, y, core) for x in range(4)] for y in range(4) for core in range(2)]


def swap_cores(block):
    return lax.ppermute(block, "dp", [(i, i ^ 1) for i in range(16)])


def swap_halves(block):
    return lax.ppermute(block, "sec", [(0, 1), (1, 0)])


def weight_to_plane():
    route = []
    for p in range(32):
        for t in range(N_TP):
            route.append((p * N_TP + t, (t * 4 + p % 4) * N_TP + p // 4))
    return route


def grad_from_plane():
    route = []
    for x in range(4):
        for y in range(4):
            for core in range(2):
                for t in range(N_TP):
                    source = plane_index(x, y, core) * N_TP + t
                    row = 4 * t + 2 * core + x // 2
                    route.append((source, row * N_TP + ((2 * y + x % 2) ^ t)))
    return route


def column_product_kernel(left_ref, right_ref, out_ref):
    out_ref[0] = jnp.dot(
        left_ref[...], right_ref[...], preferred_element_type=F32
    ).astype(out_ref.dtype)


def column_product(left, right):
    rows, depth = left.shape
    width = right.shape[1] // N_TP
    return pl.pallas_call(
        column_product_kernel,
        grid=(N_TP,),
        in_specs=[
            pl.BlockSpec((rows, depth), lambda i: (0, 0)),
            pl.BlockSpec((depth, width), lambda i: (0, i)),
        ],
        out_specs=pl.BlockSpec((1, rows, width), lambda i: (i, 0, 0)),
        out_shape=jax.ShapeDtypeStruct((N_TP, rows, width), BF),
        cost_estimate=pl.CostEstimate(
            flops=2 * rows * right.size, bytes_accessed=2 * right.size, transcendentals=0
        ),
    )(left, right)


def block_product_kernel(left_ref, right_ref, out_ref):
    out_ref[0] = jnp.dot(
        left_ref[...], right_ref[0], preferred_element_type=F32
    ).astype(out_ref.dtype)


def block_product(left, right):
    rows, depth = left.shape
    width = right.shape[2]
    return pl.pallas_call(
        block_product_kernel,
        grid=(N_TP,),
        in_specs=[
            pl.BlockSpec((rows, depth), lambda i: (0, 0)),
            pl.BlockSpec((1, depth, width), lambda i: (i, 0, 0)),
        ],
        out_specs=pl.BlockSpec((1, rows, width), lambda i: (i, 0, 0)),
        out_shape=jax.ShapeDtypeStruct((N_TP, rows, width), BF),
        cost_estimate=pl.CostEstimate(
            flops=2 * rows * right.size, bytes_accessed=2 * right.size, transcendentals=0
        ),
    )(left, right)


def block_sum_kernel(left_ref, right_ref, out_ref):
    part = lax.dot_general(
        left_ref[0], right_ref[0], (((1,), (1,)), ((), ())), preferred_element_type=F32
    )

    @pl.when(pl.program_id(0) == 0)
    def _():
        out_ref[...] = part

    @pl.when(pl.program_id(0) > 0)
    def _():
        out_ref[...] += part


def block_sum(left, right):
    rows, width = left.shape[1:]
    depth = right.shape[1]
    return pl.pallas_call(
        block_sum_kernel,
        grid=(N_TP,),
        in_specs=[
            pl.BlockSpec((1, rows, width), lambda i: (i, 0, 0)),
            pl.BlockSpec((1, depth, width), lambda i: (i, 0, 0)),
        ],
        out_specs=pl.BlockSpec((rows, depth), lambda i: (0, 0)),
        out_shape=jax.ShapeDtypeStruct((rows, depth), F32),
        cost_estimate=pl.CostEstimate(
            flops=2 * rows * right.size, bytes_accessed=2 * right.size, transcendentals=0
        ),
    )(left, right)


def line_product_kernel(normed_ref, own_ref, other_ref, out_ref):
    total = jnp.zeros((512, 512), F32)
    for side, cot_ref in enumerate((own_ref, other_ref)):
        total += lax.dot_general(
            normed_ref[:, side].reshape(512, 512),
            cot_ref[...].reshape(512, 512),
            (((0,), (0,)), ((), ())),
            preferred_element_type=F32,
        )
    for i in range(4):
        row, col = i // 2 * 256, i % 2 * 256
        out_ref[i] = total[row : row + 256, col : col + 256].astype(BF)


def line_product(normed, own, other):
    return pl.pallas_call(
        line_product_kernel,
        out_shape=jax.ShapeDtypeStruct((4, 256, 256), BF),
        cost_estimate=pl.CostEstimate(
            flops=2 * 1024 * 512 * 512, bytes_accessed=3 << 20, transcendentals=0
        ),
    )(normed, own, other)


def flip_bits(blocks, number):
    shape = blocks.shape
    blocks = blocks.reshape((2, 2, 2) + shape[1:])
    for axis in range(3):
        bit = (number >> (2 - axis)) & 1
        blocks = jnp.where(bit == 1, jnp.flip(blocks, axis), blocks)
    return blocks.reshape(shape)


def layer_norm(values, gain_vector, bias_vector):
    average = jnp.mean(values, axis=-1, keepdims=True)
    centered = values - average
    variance = jnp.mean(centered * centered, axis=-1, keepdims=True)
    return centered * lax.rsqrt(variance + 1e-06) * gain_vector + bias_vector


def exchange_tp(blocks):
    return lax.all_to_all(blocks, "tp", 0, 0)


def gather_tp(block):
    return exchange_tp(jnp.broadcast_to(block[None], (N_TP,) + block.shape))


def per_device(
    patches,
    counts,
    positions,
    pe_weight,
    ln_gain,
    ln_bias,
    w_in,
    b_in,
    w_out,
    b_out,
    text_embeds,
    rms_gain,
    kv_weight,
    kv_cotangent,
):
    sec = lax.axis_index("sec")
    dp = lax.axis_index("dp")
    tp = lax.axis_index("tp")
    core = dp % 2
    image_count = counts[(1 - sec) * 16 + dp]

    tokens = patches.shape[1] // MERGE_PATCHES
    rows = patches[0].reshape(tokens, MERGE_PATCHES, -1).transpose(1, 0, 2)
    rows = jnp.pad(rows, ((0, 0), (0, 16 - tokens), (0, 0))).reshape(MERGE_PATCHES * 16, -1)
    columns, rows = lax.optimization_barrier((pe_weight.T, rows))
    patch_all = lax.all_gather(rows, "tp", tiled=True)

    mine = lax.all_to_all(
        jnp.broadcast_to(columns[None], (16,) + columns.shape),
        PLANE,
        0,
        0,
        axis_index_groups=SAME_CORE,
    )
    other = swap_cores(mine)
    first = jnp.where(core == 0, mine, other)
    second = jnp.where(core == 0, other, mine)
    full_patch = jnp.stack([first, second], axis=1).reshape(1280, -1)

    weight_block = lax.ppermute(kv_weight, ALL, weight_to_plane())
    weight_block, cot_input, _ = lax.optimization_barrier((weight_block, kv_cotangent[0], mine))
    weight_all = lax.all_gather(weight_block, PLANE).reshape(N_TP, 1024, 256)

    cotangents = gather_tp(cot_input)
    cot_line = flip_bits(cotangents, tp)
    cot_line = cot_line.reshape(4, 2, 128, 256).transpose(0, 2, 1, 3).reshape(4, 128, 512)
    projected = lax.dot_general(
        patch_all, full_patch, (((1,), (1,)), ((), ())), preferred_element_type=F32
    )
    cot_line, projected = lax.optimization_barrier((cot_line, projected))
    cot_line = lax.all_to_all(cot_line, PLANE, 0, 0, axis_index_groups=SAME_X)
    cot_other = swap_cores(cot_line)

    embedded = layer_norm(projected, ln_gain, ln_bias).astype(BF)
    embedded = embedded.reshape(N_TP, MERGE_PATCHES, 16, 1280)
    merged = jnp.concatenate(
        [embedded[:, m].reshape(N_TP * 16, 1280) for m in range(MERGE_PATCHES)], axis=1
    )
    before_gelu = jnp.dot(merged, w_in, preferred_element_type=F32) + b_in
    hidden = jax.nn.gelu(before_gelu, approximate=False).astype(BF)
    hidden = hidden.reshape(N_TP, 16, -1)[:, :tokens].reshape(N_TP * tokens, -1)
    hidden = swap_halves(hidden)
    hidden, cot_line, cot_other = lax.optimization_barrier((hidden, cot_line, cot_other))
    partial = column_product(hidden, w_out)
    vision = (jnp.sum(exchange_tp(partial).astype(F32), axis=0) + b_out).astype(BF)

    line_index = jnp.arange(128)
    slot_positions = positions[0]
    slot_ok = jnp.arange(112) < image_count
    selector = (slot_positions[None, :] == line_index[:, None]) & slot_ok[None, :]
    selector_bf = selector.astype(BF)
    placed = jnp.dot(selector_bf, vision, preferred_element_type=F32)
    image_rows = jnp.any(selector, axis=1, keepdims=True)
    combined = jnp.where(image_rows, placed, text_embeds[0].astype(F32))

    normed_grad = block_sum(cotangents, weight_all)
    scaled = normed_grad * rms_gain
    stats = jnp.stack([jnp.sum(combined * combined, axis=1), jnp.sum(scaled * combined, axis=1)])
    stats = jnp.sum(gather_tp(stats), axis=0)
    row_scale = lax.rsqrt(stats[0] / WIDTH + 1e-06)[:, None]
    row_dot = stats[1][:, None]
    seq_grad = (
        row_scale * scaled - combined * row_scale * row_scale * row_scale * row_dot / WIDTH
    ).astype(BF)
    image_grad = lax.dot_general(
        selector_bf, seq_grad, (((0,), (0,)), ((), ())), preferred_element_type=F32
    ).astype(BF)
    vision_grad = swap_halves(image_grad)

    gained = combined * rms_gain
    normed = (gained * row_scale).astype(BF)
    keep = jnp.where(core == 0, normed[:, :512], normed[:, 512:])
    give = jnp.where(core == 0, normed[:, 512:], normed[:, :512])
    pair = jnp.stack([keep, swap_cores(give)])
    normed_line = lax.all_to_all(
        jnp.broadcast_to(pair[None], (4,) + pair.shape), PLANE, 0, 0, axis_index_groups=SAME_X
    )
    block = line_product(normed_line, cot_line, cot_other)
    block = lax.all_to_all(block, PLANE, 0, 0, axis_index_groups=SAME_Y)
    block = jnp.sum(block.astype(F32), axis=0).astype(BF)
    kv_weight_grad = lax.ppermute(block, ALL, grad_from_plane()).astype(F32)

    product = block_product(gained.astype(BF), weight_all)
    keys_values = jnp.sum(exchange_tp(product).astype(F32), axis=0)
    keys_values = (keys_values * row_scale).astype(BF)
    return (keys_values[None], seq_grad[None], vision_grad[None], kv_weight_grad)


def solution(mesh):
    return jax.shard_map(
        per_device,
        mesh=mesh,
        in_specs=(
            P(("sec", "dp"), "tp", None),
            P(),
            P(("sec", "dp"), None),
            P(None, ("sec", "dp")),
            P(),
            P(),
            P(None, "tp"),
            P("tp"),
            P("tp", None),
            P("tp"),
            P(("sec", "dp"), None, "tp"),
            P("tp"),
            P(("sec", "dp"), "tp"),
            P(("sec", "dp"), None, "tp"),
        ),
        out_specs=(
            P(("sec", "dp"), None, "tp"),
            P(("sec", "dp"), None, "tp"),
            P(("sec", "dp"), None, "tp"),
            P(("sec", "dp"), "tp"),
        ),
        check_vma=False,
    )
```

```python
import jax
import jax.numpy as jnp
from jax import lax
from jax.experimental import pallas as pl
from jax.experimental.pallas import tpu as pltpu
from jax.sharding import PartitionSpec as P

WIDTH = 8192
MERGE_PATCHES = 4
PLANE = ("sec", "dp")
ALL = ("sec", "dp", "tp")
N_TP = 8
BF = jnp.bfloat16
F32 = jnp.float32


def plane_index(x, y, core):
    return (y % 2) * 16 + x * 4 + (y // 2) * 2 + core


SAME_CORE = [
    [plane_index(x, y, core) for lo in range(2) for x in range(4) for y in (lo, lo + 2)]
    for core in range(2)
]
SAME_X = [[plane_index(x, y, core) for y in range(4)] for x in range(4) for core in range(2)]
SAME_Y = [[plane_index(x, y, core) for x in range(4)] for y in range(4) for core in range(2)]


def swap_cores(block):
    return lax.ppermute(block, "dp", [(i, i ^ 1) for i in range(16)])


def swap_halves(block):
    return lax.ppermute(block, "sec", [(0, 1), (1, 0)])


def weight_to_plane():
    route = []
    for p in range(32):
        for t in range(N_TP):
            route.append((p * N_TP + t, (t * 4 + p % 4) * N_TP + p // 4))
    return route


def grad_from_plane():
    route = []
    for x in range(4):
        for y in range(4):
            for core in range(2):
                for t in range(N_TP):
                    source = plane_index(x, y, core) * N_TP + t
                    row = 4 * t + 2 * core + x // 2
                    route.append((source, row * N_TP + ((2 * y + x % 2) ^ t)))
    return route


def share_kernel(place_ref, block_ref, out_ref):
    out_ref[0] = block_ref[...]


def take_share(weight, place):
    return pl.pallas_call(
        share_kernel,
        grid_spec=pltpu.PrefetchScalarGridSpec(
            num_scalar_prefetch=1,
            grid=(N_TP,),
            in_specs=[
                pl.BlockSpec((40, 256), lambda i, place: (place[0] // 4, 4 * i + place[0] % 4))
            ],
            out_specs=pl.BlockSpec((1, 40, 256), lambda i, place: (i, 0, 0)),
        ),
        out_shape=jax.ShapeDtypeStruct((N_TP, 40, 256), BF),
        cost_estimate=pl.CostEstimate(flops=0, bytes_accessed=640 * 512, transcendentals=0),
    )(place.astype(jnp.int32)[None], weight)


def vision_kernel(left_ref, right_ref, bias_ref, out_ref):
    right = right_ref[:, 0].reshape(left_ref.shape[1], -1)
    total = jnp.dot(left_ref[...], right, preferred_element_type=F32) + bias_ref[...]
    out_ref[...] = total.astype(BF)


def vision_product(hidden, gathered, bias):
    rows, depth = hidden.shape
    return pl.pallas_call(
        vision_kernel,
        grid=(4,),
        in_specs=[
            pl.BlockSpec((rows, depth), lambda i: (0, 0)),
            pl.BlockSpec((8, 1, 320, 256), lambda i: (0, i, 1, 0)),
            pl.BlockSpec((1, 256), lambda i: (0, i)),
        ],
        out_specs=pl.BlockSpec((rows, 256), lambda i: (0, i)),
        out_shape=jax.ShapeDtypeStruct((rows, 1024), BF),
        cost_estimate=pl.CostEstimate(
            flops=2 * rows * depth * 1024, bytes_accessed=2 * depth * 1024, transcendentals=0
        ),
    )(hidden, gathered, bias[None])


def block_product_kernel(left_ref, right_ref, out_ref):
    out_ref[0] = jnp.dot(
        left_ref[...], right_ref[0].reshape(1024, 256), preferred_element_type=F32
    ).astype(out_ref.dtype)


def block_product(left, gathered):
    rows = left.shape[0]
    return pl.pallas_call(
        block_product_kernel,
        grid=(N_TP,),
        in_specs=[
            pl.BlockSpec((rows, 1024), lambda i: (0, 0)),
            pl.BlockSpec((1, 4, 256, 256), lambda i: (i, 0, 0, 0)),
        ],
        out_specs=pl.BlockSpec((1, rows, 256), lambda i: (i, 0, 0)),
        out_shape=jax.ShapeDtypeStruct((N_TP, rows, 256), BF),
        cost_estimate=pl.CostEstimate(
            flops=2 * rows * 1024 * 2048, bytes_accessed=4 << 20, transcendentals=0
        ),
    )(left, gathered)


def block_sum_kernel(left_ref, right_ref, out_ref, total_ref):
    step = pl.program_id(0)
    part = lax.dot_general(
        right_ref[0].reshape(1024, 256),
        left_ref[0],
        (((1,), (1,)), ((), ())),
        preferred_element_type=F32,
    )

    @pl.when(step == 0)
    def _():
        total_ref[...] = part

    @pl.when(step > 0)
    def _():
        total_ref[...] += part

    @pl.when(step == N_TP - 1)
    def _():
        out_ref[...] = total_ref[...].T


def block_sum(left, gathered):
    rows = left.shape[1]
    return pl.pallas_call(
        block_sum_kernel,
        grid=(N_TP,),
        in_specs=[
            pl.BlockSpec((1, rows, 256), lambda i: (i, 0, 0)),
            pl.BlockSpec((1, 4, 256, 256), lambda i: (i, 0, 0, 0)),
        ],
        out_specs=pl.BlockSpec((rows, 1024), lambda i: (0, 0)),
        out_shape=jax.ShapeDtypeStruct((rows, 1024), F32),
        scratch_shapes=[pltpu.VMEM((1024, rows), F32)],
        cost_estimate=pl.CostEstimate(
            flops=2 * rows * 1024 * 2048, bytes_accessed=4 << 20, transcendentals=0
        ),
    )(left, gathered)


def line_product_kernel(normed_ref, own_ref, other_ref, out_ref):
    total = jnp.zeros((512, 512), F32)
    for side, cot_ref in enumerate((own_ref, other_ref)):
        total += lax.dot_general(
            normed_ref[:, side].reshape(512, 512),
            cot_ref[...].reshape(512, 512),
            (((0,), (0,)), ((), ())),
            preferred_element_type=F32,
        )
    for i in range(4):
        row, col = i // 2 * 256, i % 2 * 256
        out_ref[i] = total[row : row + 256, col : col + 256].astype(BF)


def line_product(normed, own, other):
    return pl.pallas_call(
        line_product_kernel,
        out_shape=jax.ShapeDtypeStruct((4, 256, 256), BF),
        cost_estimate=pl.CostEstimate(
            flops=2 * 1024 * 512 * 512, bytes_accessed=3 << 20, transcendentals=0
        ),
    )(normed, own, other)


def flip_bits(blocks, number):
    shape = blocks.shape
    blocks = blocks.reshape((2, 2, 2) + shape[1:])
    for axis in range(3):
        bit = (number >> (2 - axis)) & 1
        blocks = jnp.where(bit == 1, jnp.flip(blocks, axis), blocks)
    return blocks.reshape(shape)


def layer_norm(values, gain_vector, bias_vector):
    average = jnp.mean(values, axis=-1, keepdims=True)
    centered = values - average
    variance = jnp.mean(centered * centered, axis=-1, keepdims=True)
    return centered * lax.rsqrt(variance + 1e-06) * gain_vector + bias_vector


def exchange_tp(blocks):
    return lax.all_to_all(blocks, "tp", 0, 0)


def gather_tp(block):
    return exchange_tp(jnp.broadcast_to(block[None], (N_TP,) + block.shape))


def per_device(
    patches,
    counts,
    positions,
    pe_weight,
    ln_gain,
    ln_bias,
    w_in,
    b_in,
    w_out,
    b_out,
    text_embeds,
    rms_gain,
    kv_weight,
    kv_cotangent,
):
    sec = lax.axis_index("sec")
    dp = lax.axis_index("dp")
    tp = lax.axis_index("tp")
    core = dp % 2
    image_count = counts[(1 - sec) * 16 + dp]

    tokens = patches.shape[1] // MERGE_PATCHES
    rows = patches[0].reshape(tokens, MERGE_PATCHES, -1).transpose(1, 0, 2)
    rows = jnp.pad(rows, ((0, 0), (0, 16 - tokens), (0, 0))).reshape(MERGE_PATCHES * 16, -1)
    patch_all = lax.all_gather(rows, "tp", tiled=True)

    columns = pe_weight.T
    mine = lax.all_to_all(
        jnp.broadcast_to(columns[None], (16,) + columns.shape),
        PLANE,
        0,
        0,
        axis_index_groups=SAME_CORE,
    )
    place = sec * 16 + dp
    weight_block = lax.ppermute(kv_weight, ALL, weight_to_plane())
    share, weight_block, mine = lax.optimization_barrier(
        (take_share(w_out, place), weight_block, mine)
    )
    share = exchange_tp(share).reshape(320, 256)

    shard = jnp.concatenate([weight_block, jnp.zeros((64, 256), BF), share], axis=0)
    gathered = lax.all_gather(shard, PLANE).reshape(8, 4, 640, 256)

    cot_input, _ = lax.optimization_barrier((kv_cotangent[0], share))
    cotangents = gather_tp(cot_input)
    other = swap_cores(mine)
    first = jnp.where(core == 0, mine, other)
    second = jnp.where(core == 0, other, mine)
    full_patch = jnp.stack([first, second], axis=1).reshape(1280, -1)
    projected = lax.dot_general(
        patch_all, full_patch, (((1,), (1,)), ((), ())), preferred_element_type=F32
    )
    embedded = layer_norm(projected, ln_gain, ln_bias).astype(BF)
    embedded = embedded.reshape(N_TP, MERGE_PATCHES, 16, 1280)
    merged = jnp.concatenate(
        [embedded[:, m].reshape(N_TP * 16, 1280) for m in range(MERGE_PATCHES)], axis=1
    )
    before_gelu = jnp.dot(merged, w_in, preferred_element_type=F32) + b_in
    hidden = jax.nn.gelu(before_gelu, approximate=False).astype(BF)
    hidden = hidden.reshape(N_TP, 16, -1)[:, :tokens].reshape(N_TP * tokens, -1)
    hidden = swap_halves(hidden).T
    hidden, cotangents = lax.optimization_barrier((hidden, cotangents))
    hidden = gather_tp(hidden)

    cot_line = flip_bits(cotangents, tp)
    cot_line = cot_line.reshape(4, 2, 128, 256).transpose(0, 2, 1, 3).reshape(4, 128, 512)
    cot_line, hidden = lax.optimization_barrier((cot_line, hidden))
    cot_line = lax.all_to_all(cot_line, PLANE, 0, 0, axis_index_groups=SAME_X)
    cot_other = swap_cores(cot_line)

    hidden = hidden.reshape(N_TP, 8, 40, -1).transpose(1, 0, 2, 3).reshape(2560, -1).T
    vision = vision_product(hidden, gathered, b_out)

    line_index = jnp.arange(128)
    slot_positions = positions[0]
    slot_ok = jnp.arange(112) < image_count
    selector = (slot_positions[None, :] == line_index[:, None]) & slot_ok[None, :]
    selector_bf = selector.astype(BF)
    placed = jnp.dot(selector_bf, vision, preferred_element_type=F32)
    image_rows = jnp.any(selector, axis=1, keepdims=True)
    combined = jnp.where(image_rows, placed, text_embeds[0].astype(F32))

    normed_grad = block_sum(cotangents, gathered)
    scaled = normed_grad * rms_gain
    stats = jnp.stack([jnp.sum(combined * combined, axis=1), jnp.sum(scaled * combined, axis=1)])
    stats, cot_line, cot_other = lax.optimization_barrier((stats, cot_line, cot_other))
    stats = jnp.sum(gather_tp(stats), axis=0)
    row_scale = lax.rsqrt(stats[0] / WIDTH + 1e-06)[:, None]
    row_dot = stats[1][:, None]
    seq_grad = (
        row_scale * scaled - combined * row_scale * row_scale * row_scale * row_dot / WIDTH
    ).astype(BF)
    image_grad = lax.dot_general(
        selector_bf, seq_grad, (((0,), (0,)), ((), ())), preferred_element_type=F32
    ).astype(BF)
    vision_grad = swap_halves(image_grad)

    gained = combined * rms_gain
    normed = (gained * row_scale).astype(BF)
    keep = jnp.where(core == 0, normed[:, :512], normed[:, 512:])
    give = jnp.where(core == 0, normed[:, 512:], normed[:, :512])
    pair = jnp.stack([keep, swap_cores(give)])
    normed_line = lax.all_to_all(
        jnp.broadcast_to(pair[None], (4,) + pair.shape), PLANE, 0, 0, axis_index_groups=SAME_X
    )
    block = line_product(normed_line, cot_line, cot_other)
    block = lax.all_to_all(block, PLANE, 0, 0, axis_index_groups=SAME_Y)
    product = block_product(gained.astype(BF), gathered)
    block = jnp.sum(block.astype(F32), axis=0).astype(BF)
    product, block = lax.optimization_barrier((product, block))
    kv_weight_grad = lax.ppermute(block, ALL, grad_from_plane()).astype(F32)
    keys_values = jnp.sum(exchange_tp(product).astype(F32), axis=0)
    keys_values = (keys_values * row_scale).astype(BF)
    return (keys_values[None], seq_grad[None], vision_grad[None], kv_weight_grad)


def solution(mesh):
    return jax.shard_map(
        per_device,
        mesh=mesh,
        in_specs=(
            P(("sec", "dp"), "tp", None),
            P(),
            P(("sec", "dp"), None),
            P(None, ("sec", "dp")),
            P(),
            P(),
            P(None, "tp"),
            P("tp"),
            P("tp", None),
            P("tp"),
            P(("sec", "dp"), None, "tp"),
            P("tp"),
            P(("sec", "dp"), "tp"),
            P(("sec", "dp"), None, "tp"),
        ),
        out_specs=(
            P(("sec", "dp"), None, "tp"),
            P(("sec", "dp"), None, "tp"),
            P(("sec", "dp"), None, "tp"),
            P(("sec", "dp"), "tp"),
        ),
        check_vma=False,
    )
```

```python
import jax
import jax.numpy as jnp
from jax import lax
from jax.experimental import pallas as pl
from jax.experimental.pallas import tpu as pltpu
from jax.sharding import PartitionSpec as P

WIDTH = 8192
MERGE_PATCHES = 4
PLANE = ("sec", "dp")
ALL = ("sec", "dp", "tp")
N_TP = 8
BF = jnp.bfloat16
F32 = jnp.float32


def plane_index(x, y, core):
    return (y % 2) * 16 + x * 4 + (y // 2) * 2 + core


SAME_CORE = [
    [plane_index(x, y, core) for lo in range(2) for x in range(4) for y in (lo, lo + 2)]
    for core in range(2)
]
SAME_X = [[plane_index(x, y, core) for y in range(4) for core in range(2)] for x in range(4)]
SAME_Y = [[plane_index(x, y, core) for x in range(4)] for y in range(4) for core in range(2)]


def swap_cores(block):
    return lax.ppermute(block, "dp", [(i, i ^ 1) for i in range(16)])


def swap_halves(block):
    return lax.ppermute(block, "sec", [(0, 1), (1, 0)])


def weight_to_plane():
    route = []
    for p in range(32):
        for t in range(N_TP):
            plane = p // 4
            route.append((p * N_TP + t, ((t ^ plane) * 4 + p % 4) * N_TP + plane))
    return route


def grad_from_plane():
    route = []
    for x in range(4):
        for y in range(4):
            for core in range(2):
                for t in range(N_TP):
                    source = plane_index(x, y, core) * N_TP + t
                    row = 4 * t + 2 * core + x // 2
                    route.append((source, row * N_TP + ((2 * y + x % 2) ^ t)))
    return route


def share_kernel(place_ref, block_ref, out_ref):
    out_ref[0] = block_ref[...]


def take_share(weight, place):
    return pl.pallas_call(
        share_kernel,
        grid_spec=pltpu.PrefetchScalarGridSpec(
            num_scalar_prefetch=1,
            grid=(N_TP,),
            in_specs=[
                pl.BlockSpec((40, 256), lambda i, place: (place[0] // 4, 4 * i + place[0] % 4))
            ],
            out_specs=pl.BlockSpec((1, 40, 256), lambda i, place: (i, 0, 0)),
        ),
        out_shape=jax.ShapeDtypeStruct((N_TP, 40, 256), BF),
        cost_estimate=pl.CostEstimate(flops=0, bytes_accessed=640 * 512, transcendentals=0),
    )(place.astype(jnp.int32)[None], weight)


def vision_kernel(left_ref, right_ref, bias_ref, out_ref):
    right = right_ref[:, 0].reshape(left_ref.shape[1], -1)
    total = jnp.dot(left_ref[...], right, preferred_element_type=F32) + bias_ref[...]
    out_ref[...] = total.astype(BF)


def vision_product(hidden, gathered, bias):
    rows, depth = hidden.shape
    return pl.pallas_call(
        vision_kernel,
        grid=(4,),
        in_specs=[
            pl.BlockSpec((rows, depth), lambda i: (0, 0)),
            pl.BlockSpec((8, 1, 320, 256), lambda i: (0, i, 1, 0)),
            pl.BlockSpec((1, 256), lambda i: (0, i)),
        ],
        out_specs=pl.BlockSpec((rows, 256), lambda i: (0, i)),
        out_shape=jax.ShapeDtypeStruct((rows, 1024), BF),
        cost_estimate=pl.CostEstimate(
            flops=2 * rows * depth * 1024, bytes_accessed=2 * depth * 1024, transcendentals=0
        ),
    )(hidden, gathered, bias[None])


def block_product_kernel(plane_ref, left_ref, right_ref, out_ref):
    out_ref[0] = jnp.dot(
        left_ref[...], right_ref[0].reshape(1024, 256), preferred_element_type=F32
    )


def block_product(left, gathered, plane):
    rows = left.shape[0]
    return pl.pallas_call(
        block_product_kernel,
        grid_spec=pltpu.PrefetchScalarGridSpec(
            num_scalar_prefetch=1,
            grid=(N_TP,),
            in_specs=[
                pl.BlockSpec((rows, 1024), lambda i, plane: (0, 0)),
                pl.BlockSpec((1, 4, 256, 256), lambda i, plane: (i, 0, 0, 0)),
            ],
            out_specs=pl.BlockSpec((1, rows, 256), lambda i, plane: (i ^ plane[0], 0, 0)),
        ),
        out_shape=jax.ShapeDtypeStruct((N_TP, rows, 256), F32),
        cost_estimate=pl.CostEstimate(
            flops=2 * rows * 1024 * 2048, bytes_accessed=4 << 20, transcendentals=0
        ),
    )(plane.astype(jnp.int32)[None], left, gathered)


def block_sum_kernel(left_ref, right_ref, out_ref):
    total = jnp.zeros(out_ref.shape, F32)
    for t in range(N_TP):
        total += lax.dot_general(
            left_ref[t],
            right_ref[t, 0],
            (((1,), (1,)), ((), ())),
            preferred_element_type=F32,
        )
    out_ref[...] = total


def block_sum(left, gathered):
    rows = left.shape[1]
    return pl.pallas_call(
        block_sum_kernel,
        grid=(4,),
        in_specs=[
            pl.BlockSpec((N_TP, rows, 256), lambda i: (0, 0, 0)),
            pl.BlockSpec((N_TP, 1, 256, 256), lambda i: (0, i, 0, 0)),
        ],
        out_specs=pl.BlockSpec((rows, 256), lambda i: (0, i)),
        out_shape=jax.ShapeDtypeStruct((rows, 1024), F32),
        cost_estimate=pl.CostEstimate(
            flops=2 * rows * 1024 * 2048, bytes_accessed=4 << 20, transcendentals=0
        ),
    )(left, gathered)


def line_product_kernel(normed_ref, cot_ref, out_ref):
    total = lax.dot_general(
        normed_ref[...].reshape(1024, 512),
        cot_ref[...].reshape(1024, 512),
        (((0,), (0,)), ((), ())),
        preferred_element_type=F32,
    )
    for i in range(4):
        row, col = i // 2 * 256, i % 2 * 256
        out_ref[i] = total[row : row + 256, col : col + 256].astype(BF)


def line_product(normed, cotangents):
    return pl.pallas_call(
        line_product_kernel,
        out_shape=jax.ShapeDtypeStruct((4, 256, 256), BF),
        cost_estimate=pl.CostEstimate(
            flops=2 * 1024 * 512 * 512, bytes_accessed=3 << 20, transcendentals=0
        ),
    )(normed, cotangents)


def flip_bits(blocks, number):
    shape = blocks.shape
    blocks = blocks.reshape((2, 2, 2) + shape[1:])
    for axis in range(3):
        bit = (number >> (2 - axis)) & 1
        blocks = jnp.where(bit == 1, jnp.flip(blocks, axis), blocks)
    return blocks.reshape(shape)


def layer_norm(values, gain_vector, bias_vector):
    average = jnp.mean(values, axis=-1, keepdims=True)
    centered = values - average
    variance = jnp.mean(centered * centered, axis=-1, keepdims=True)
    return centered * lax.rsqrt(variance + 1e-06) * gain_vector + bias_vector


def exchange_tp(blocks):
    return lax.all_to_all(blocks, "tp", 0, 0)


def gather_tp(block):
    return exchange_tp(jnp.broadcast_to(block[None], (N_TP,) + block.shape))


def per_device(
    patches,
    counts,
    positions,
    pe_weight,
    ln_gain,
    ln_bias,
    w_in,
    b_in,
    w_out,
    b_out,
    text_embeds,
    rms_gain,
    kv_weight,
    kv_cotangent,
):
    sec = lax.axis_index("sec")
    dp = lax.axis_index("dp")
    tp = lax.axis_index("tp")
    core = dp % 2
    image_count = counts[(1 - sec) * 16 + dp]

    tokens = patches.shape[1] // MERGE_PATCHES
    rows = patches[0].reshape(tokens, MERGE_PATCHES, -1).transpose(1, 0, 2)
    rows = jnp.pad(rows, ((0, 0), (0, 16 - tokens), (0, 0))).reshape(MERGE_PATCHES * 16, -1)
    patch_all = lax.all_gather(rows, "tp", tiled=True)

    place = sec * 16 + dp
    weight_block = lax.ppermute(kv_weight, ALL, weight_to_plane())
    share = exchange_tp(take_share(w_out, place)).reshape(320, 256)

    columns, _ = lax.optimization_barrier((pe_weight.T, share))
    mine = lax.all_to_all(
        jnp.broadcast_to(columns[None], (16,) + columns.shape),
        PLANE,
        0,
        0,
        axis_index_groups=SAME_CORE,
    )
    shard = jnp.concatenate([weight_block, jnp.zeros((64, 256), BF), share], axis=0)
    gathered = lax.all_gather(shard, PLANE).reshape(8, 4, 640, 256)

    cot_input, mine = lax.optimization_barrier((kv_cotangent[0], mine))
    cotangents = gather_tp(cot_input)
    other = swap_cores(mine)
    first = jnp.where(core == 0, mine, other)
    second = jnp.where(core == 0, other, mine)
    full_patch = jnp.stack([first, second], axis=1).reshape(1280, -1)
    projected = lax.dot_general(
        patch_all, full_patch, (((1,), (1,)), ((), ())), preferred_element_type=F32
    )
    embedded = layer_norm(projected, ln_gain, ln_bias).astype(BF)
    embedded = embedded.reshape(N_TP, MERGE_PATCHES, 16, 1280)
    merged = jnp.concatenate(
        [embedded[:, m].reshape(N_TP * 16, 1280) for m in range(MERGE_PATCHES)], axis=1
    )
    before_gelu = jnp.dot(merged, w_in, preferred_element_type=F32) + b_in
    hidden = jax.nn.gelu(before_gelu, approximate=False).astype(BF)
    hidden = hidden.reshape(N_TP, 16, -1)[:, :tokens].reshape(N_TP * tokens, -1)
    hidden = swap_halves(hidden).T
    hidden, cotangents = lax.optimization_barrier((hidden, cotangents))
    hidden = gather_tp(hidden)

    cotangents = flip_bits(cotangents, tp)
    cot_line = cotangents
    cot_line = cot_line.reshape(4, 1, 2, 128, 256).transpose(0, 1, 3, 2, 4)
    cot_line = jnp.broadcast_to(cot_line, (4, 2, 128, 2, 256)).reshape(8, 128, 512)
    cot_line, hidden = lax.optimization_barrier((cot_line, hidden))
    cot_line = lax.all_to_all(cot_line, PLANE, 0, 0, axis_index_groups=SAME_X)

    hidden = hidden.reshape(N_TP, 8, 40, -1).transpose(1, 0, 2, 3).reshape(2560, -1).T
    vision = vision_product(hidden, gathered, b_out)

    line_index = jnp.arange(128)
    slot_positions = positions[0]
    slot_ok = jnp.arange(112) < image_count
    selector = (slot_positions[None, :] == line_index[:, None]) & slot_ok[None, :]
    selector_bf = selector.astype(BF)
    placed = jnp.dot(selector_bf, vision, preferred_element_type=F32)
    image_rows = jnp.any(selector, axis=1, keepdims=True)
    combined = jnp.where(image_rows, placed, text_embeds[0].astype(F32))

    normed_grad = block_sum(cotangents, gathered)
    scaled = normed_grad * rms_gain
    stats = jnp.stack([jnp.sum(combined * combined, axis=1), jnp.sum(scaled * combined, axis=1)])
    stats, cot_line = lax.optimization_barrier((stats, cot_line))
    stats = jnp.sum(gather_tp(stats), axis=0)
    row_scale = lax.rsqrt(stats[0] / WIDTH + 1e-06)[:, None]
    row_dot = stats[1][:, None]

    gained = combined * rms_gain
    product = block_product(gained.astype(BF), gathered, tp)
    row_scale, product = lax.optimization_barrier((row_scale, product))
    normed = (gained * row_scale).astype(BF)
    normed = normed.reshape(128, 2, 512).transpose(1, 0, 2)
    normed_line = lax.all_to_all(
        jnp.broadcast_to(normed[None], (4, 2, 128, 512)).reshape(8, 128, 512),
        PLANE,
        0,
        0,
        axis_index_groups=SAME_X,
    )
    block = line_product(normed_line, cot_line)
    block = lax.all_to_all(block, PLANE, 0, 0, axis_index_groups=SAME_Y)
    block = jnp.sum(block.astype(F32), axis=0).astype(BF)
    kv_weight_grad = lax.ppermute(block, ALL, grad_from_plane()).astype(F32)

    keys_values = lax.psum_scatter(product, "tp", scatter_dimension=0, tiled=True)[0]
    keys_values = (keys_values * row_scale).astype(BF)

    seq_grad = (
        row_scale * scaled - combined * row_scale * row_scale * row_scale * row_dot / WIDTH
    ).astype(BF)
    image_grad = lax.dot_general(
        selector_bf, seq_grad, (((0,), (0,)), ((), ())), preferred_element_type=F32
    ).astype(BF)
    vision_grad = swap_halves(image_grad)
    return (keys_values[None], seq_grad[None], vision_grad[None], kv_weight_grad)


def solution(mesh):
    return jax.shard_map(
        per_device,
        mesh=mesh,
        in_specs=(
            P(("sec", "dp"), "tp", None),
            P(),
            P(("sec", "dp"), None),
            P(None, ("sec", "dp")),
            P(),
            P(),
            P(None, "tp"),
            P("tp"),
            P("tp", None),
            P("tp"),
            P(("sec", "dp"), None, "tp"),
            P("tp"),
            P(("sec", "dp"), "tp"),
            P(("sec", "dp"), None, "tp"),
        ),
        out_specs=(
            P(("sec", "dp"), None, "tp"),
            P(("sec", "dp"), None, "tp"),
            P(("sec", "dp"), None, "tp"),
            P(("sec", "dp"), "tp"),
        ),
        check_vma=False,
    )
```

```python
import jax
import jax.numpy as jnp
from jax import lax
from jax.experimental import pallas as pl
from jax.experimental.pallas import tpu as pltpu
from jax.sharding import PartitionSpec as P

WIDTH = 8192
MERGE_PATCHES = 4
PLANE = ("sec", "dp")
ALL = ("sec", "dp", "tp")
N_TP = 8
BF = jnp.bfloat16
F32 = jnp.float32


def plane_index(x, y, core):
    return (y % 2) * 16 + x * 4 + (y // 2) * 2 + core


SAME_CORE = [
    [plane_index(x, y, core) for lo in range(2) for x in range(4) for y in (lo, lo + 2)]
    for core in range(2)
]
SAME_X = [[plane_index(x, y, core) for y in range(4) for core in range(2)] for x in range(4)]
SAME_Y = [[plane_index(x, y, core) for x in range(4)] for y in range(4) for core in range(2)]


def swap_cores(block):
    return lax.ppermute(block, "dp", [(i, i ^ 1) for i in range(16)])


def swap_halves(block):
    return lax.ppermute(block, "sec", [(0, 1), (1, 0)])


def weight_to_plane():
    route = []
    for p in range(32):
        for t in range(N_TP):
            plane = p // 4
            route.append((p * N_TP + t, ((t ^ plane) * 4 + p % 4) * N_TP + plane))
    return route


def grad_from_plane():
    route = []
    for x in range(4):
        for y in range(4):
            for core in range(2):
                for t in range(N_TP):
                    source = plane_index(x, y, core) * N_TP + t
                    row = 4 * t + 2 * core + x // 2
                    route.append((source, row * N_TP + ((2 * y + x % 2) ^ t)))
    return route


def share_kernel(place_ref, block_ref, out_ref):
    out_ref[0] = block_ref[...]


def take_share(weight, place):
    return pl.pallas_call(
        share_kernel,
        grid_spec=pltpu.PrefetchScalarGridSpec(
            num_scalar_prefetch=1,
            grid=(N_TP,),
            in_specs=[
                pl.BlockSpec((40, 256), lambda i, place: (place[0] // 4, 4 * i + place[0] % 4))
            ],
            out_specs=pl.BlockSpec((1, 40, 256), lambda i, place: (i, 0, 0)),
        ),
        out_shape=jax.ShapeDtypeStruct((N_TP, 40, 256), BF),
        cost_estimate=pl.CostEstimate(flops=0, bytes_accessed=640 * 512, transcendentals=0),
    )(place.astype(jnp.int32)[None], weight)


def vision_kernel(left_ref, most_ref, rest_ref, bias_ref, out_ref):
    most = most_ref[:, 0].reshape(2048, 256)
    rest = rest_ref[:, 0].reshape(512, 256)
    total = jnp.dot(left_ref[:, :2048], most, preferred_element_type=F32)
    total += jnp.dot(left_ref[:, 2048:], rest, preferred_element_type=F32)
    out_ref[...] = (total + bias_ref[...]).astype(BF)


def vision_product(hidden, gathered, bias):
    rows, depth = hidden.shape
    return pl.pallas_call(
        vision_kernel,
        grid=(4,),
        in_specs=[
            pl.BlockSpec((rows, depth), lambda i: (0, 0)),
            pl.BlockSpec((8, 1, 256, 256), lambda i: (0, i, 1, 0)),
            pl.BlockSpec((8, 1, 64, 256), lambda i: (0, i, 8, 0)),
            pl.BlockSpec((1, 256), lambda i: (0, i)),
        ],
        out_specs=pl.BlockSpec((rows, 256), lambda i: (0, i)),
        out_shape=jax.ShapeDtypeStruct((rows, 1024), BF),
        cost_estimate=pl.CostEstimate(
            flops=2 * rows * depth * 1024, bytes_accessed=2 * depth * 1024, transcendentals=0
        ),
    )(hidden, gathered, gathered, bias[None])


def block_product_kernel(plane_ref, left_ref, right_ref, out_ref):
    out_ref[0] = jnp.dot(
        left_ref[...], right_ref[0].reshape(1024, 256), preferred_element_type=F32
    )


def block_product(left, gathered, plane):
    rows = left.shape[0]
    return pl.pallas_call(
        block_product_kernel,
        grid_spec=pltpu.PrefetchScalarGridSpec(
            num_scalar_prefetch=1,
            grid=(N_TP,),
            in_specs=[
                pl.BlockSpec((rows, 1024), lambda i, plane: (0, 0)),
                pl.BlockSpec((1, 4, 256, 256), lambda i, plane: (i, 0, 0, 0)),
            ],
            out_specs=pl.BlockSpec((1, rows, 256), lambda i, plane: (i ^ plane[0], 0, 0)),
        ),
        out_shape=jax.ShapeDtypeStruct((N_TP, rows, 256), F32),
        cost_estimate=pl.CostEstimate(
            flops=2 * rows * 1024 * 2048, bytes_accessed=4 << 20, transcendentals=0
        ),
    )(plane.astype(jnp.int32)[None], left, gathered)


def block_sum_kernel(left_ref, right_ref, out_ref):
    total = jnp.zeros(out_ref.shape, F32)
    for t in range(N_TP):
        total += lax.dot_general(
            left_ref[t],
            right_ref[t, 0],
            (((1,), (1,)), ((), ())),
            preferred_element_type=F32,
        )
    out_ref[...] = total


def block_sum(left, gathered):
    rows = left.shape[1]
    return pl.pallas_call(
        block_sum_kernel,
        grid=(4,),
        in_specs=[
            pl.BlockSpec((N_TP, rows, 256), lambda i: (0, 0, 0)),
            pl.BlockSpec((N_TP, 1, 256, 256), lambda i: (0, i, 0, 0)),
        ],
        out_specs=pl.BlockSpec((rows, 256), lambda i: (0, i)),
        out_shape=jax.ShapeDtypeStruct((rows, 1024), F32),
        cost_estimate=pl.CostEstimate(
            flops=2 * rows * 1024 * 2048, bytes_accessed=4 << 20, transcendentals=0
        ),
    )(left, gathered)


def line_product_kernel(normed_ref, cot_ref, out_ref):
    total = lax.dot_general(
        normed_ref[...].reshape(1024, 512),
        cot_ref[...].reshape(1024, 512),
        (((0,), (0,)), ((), ())),
        preferred_element_type=F32,
    )
    for i in range(4):
        row, col = i // 2 * 256, i % 2 * 256
        out_ref[i] = total[row : row + 256, col : col + 256].astype(BF)


def line_product(normed, cotangents):
    return pl.pallas_call(
        line_product_kernel,
        out_shape=jax.ShapeDtypeStruct((4, 256, 256), BF),
        cost_estimate=pl.CostEstimate(
            flops=2 * 1024 * 512 * 512, bytes_accessed=3 << 20, transcendentals=0
        ),
    )(normed, cotangents)


def flip_bits(blocks, number):
    shape = blocks.shape
    blocks = blocks.reshape((2, 2, 2) + shape[1:])
    for axis in range(3):
        bit = (number >> (2 - axis)) & 1
        blocks = jnp.where(bit == 1, jnp.flip(blocks, axis), blocks)
    return blocks.reshape(shape)


def layer_norm(values, gain_vector, bias_vector):
    average = jnp.mean(values, axis=-1, keepdims=True)
    centered = values - average
    variance = jnp.mean(centered * centered, axis=-1, keepdims=True)
    return centered * lax.rsqrt(variance + 1e-06) * gain_vector + bias_vector


def exchange_tp(blocks):
    return lax.all_to_all(blocks, "tp", 0, 0)


def gather_tp(block):
    return exchange_tp(jnp.broadcast_to(block[None], (N_TP,) + block.shape))


def per_device(
    patches,
    counts,
    positions,
    pe_weight,
    ln_gain,
    ln_bias,
    w_in,
    b_in,
    w_out,
    b_out,
    text_embeds,
    rms_gain,
    kv_weight,
    kv_cotangent,
):
    sec = lax.axis_index("sec")
    dp = lax.axis_index("dp")
    tp = lax.axis_index("tp")
    core = dp % 2
    image_count = counts[(1 - sec) * 16 + dp]

    tokens = patches.shape[1] // MERGE_PATCHES
    rows = patches[0].reshape(tokens, MERGE_PATCHES, -1).transpose(1, 0, 2)
    rows = jnp.pad(rows, ((0, 0), (0, 16 - tokens), (0, 0))).reshape(MERGE_PATCHES * 16, -1)
    patch_all = lax.all_gather(rows, "tp", tiled=True)

    place = sec * 16 + dp
    weight_block = lax.ppermute(kv_weight, ALL, weight_to_plane())
    share = exchange_tp(take_share(w_out, place)).reshape(320, 256)

    columns, _ = lax.optimization_barrier((pe_weight.T, share))
    mine = lax.all_to_all(
        jnp.broadcast_to(columns[None], (16,) + columns.shape),
        PLANE,
        0,
        0,
        axis_index_groups=SAME_CORE,
    )
    shard = jnp.concatenate([weight_block, share], axis=0)
    gathered = lax.all_gather(shard, PLANE).reshape(8, 4, 576, 256)

    cot_input, mine = lax.optimization_barrier((kv_cotangent[0], mine))
    cotangents = gather_tp(cot_input)
    other = swap_cores(mine)
    first = jnp.where(core == 0, mine, other)
    second = jnp.where(core == 0, other, mine)
    full_patch = jnp.stack([first, second], axis=1).reshape(1280, -1)
    projected = lax.dot_general(
        patch_all, full_patch, (((1,), (1,)), ((), ())), preferred_element_type=F32
    )
    embedded = layer_norm(projected, ln_gain, ln_bias).astype(BF)
    embedded = embedded.reshape(N_TP, MERGE_PATCHES, 16, 1280)
    merged = jnp.concatenate(
        [embedded[:, m].reshape(N_TP * 16, 1280) for m in range(MERGE_PATCHES)], axis=1
    )
    before_gelu = jnp.dot(merged, w_in, preferred_element_type=F32) + b_in
    hidden = jax.nn.gelu(before_gelu, approximate=False).astype(BF)
    hidden = hidden.reshape(N_TP, 16, -1)[:, :tokens].reshape(N_TP * tokens, -1)
    hidden = swap_halves(hidden).T
    hidden, cotangents = lax.optimization_barrier((hidden, cotangents))
    hidden = gather_tp(hidden)

    cotangents = flip_bits(cotangents, tp)
    cot_line = cotangents
    cot_line = cot_line.reshape(4, 1, 2, 128, 256).transpose(0, 1, 3, 2, 4)
    cot_line = jnp.broadcast_to(cot_line, (4, 2, 128, 2, 256)).reshape(8, 128, 512)
    cot_line, hidden = lax.optimization_barrier((cot_line, hidden))
    cot_line = lax.all_to_all(cot_line, PLANE, 0, 0, axis_index_groups=SAME_X)

    hidden = hidden.reshape(N_TP, 8, 40, -1).transpose(1, 0, 2, 3).reshape(8, 320, -1)
    hidden = jnp.concatenate(
        [hidden[:, :256].reshape(2048, -1), hidden[:, 256:].reshape(512, -1)], axis=0
    ).T
    vision = vision_product(hidden, gathered, b_out)

    line_index = jnp.arange(128)
    slot_positions = positions[0]
    slot_ok = jnp.arange(112) < image_count
    selector = (slot_positions[None, :] == line_index[:, None]) & slot_ok[None, :]
    selector_bf = selector.astype(BF)
    placed = jnp.dot(selector_bf, vision, preferred_element_type=F32)
    image_rows = jnp.any(selector, axis=1, keepdims=True)
    combined = jnp.where(image_rows, placed, text_embeds[0].astype(F32))

    normed_grad = block_sum(cotangents, gathered)
    scaled = normed_grad * rms_gain
    stats = jnp.stack([jnp.sum(combined * combined, axis=1), jnp.sum(scaled * combined, axis=1)])
    stats, cot_line = lax.optimization_barrier((stats, cot_line))
    stats = jnp.sum(gather_tp(stats), axis=0)
    row_scale = lax.rsqrt(stats[0] / WIDTH + 1e-06)[:, None]
    row_dot = stats[1][:, None]

    gained = combined * rms_gain
    product = block_product(gained.astype(BF), gathered, tp)
    row_scale, product = lax.optimization_barrier((row_scale, product))
    normed = (gained * row_scale).astype(BF)
    normed = normed.reshape(128, 2, 512).transpose(1, 0, 2)
    normed_line = lax.all_to_all(
        jnp.broadcast_to(normed[None], (4, 2, 128, 512)).reshape(8, 128, 512),
        PLANE,
        0,
        0,
        axis_index_groups=SAME_X,
    )
    block = line_product(normed_line, cot_line)
    block = lax.all_to_all(block, PLANE, 0, 0, axis_index_groups=SAME_Y)
    block = jnp.sum(block.astype(F32), axis=0).astype(BF)
    kv_weight_grad = lax.ppermute(block, ALL, grad_from_plane()).astype(F32)

    keys_values = lax.psum_scatter(product, "tp", scatter_dimension=0, tiled=True)[0]
    keys_values = (keys_values * row_scale).astype(BF)

    seq_grad = (
        row_scale * scaled - combined * row_scale * row_scale * row_scale * row_dot / WIDTH
    ).astype(BF)
    image_grad = lax.dot_general(
        selector_bf, seq_grad, (((0,), (0,)), ((), ())), preferred_element_type=F32
    ).astype(BF)
    vision_grad = swap_halves(image_grad)
    return (keys_values[None], seq_grad[None], vision_grad[None], kv_weight_grad)


def solution(mesh):
    return jax.shard_map(
        per_device,
        mesh=mesh,
        in_specs=(
            P(("sec", "dp"), "tp", None),
            P(),
            P(("sec", "dp"), None),
            P(None, ("sec", "dp")),
            P(),
            P(),
            P(None, "tp"),
            P("tp"),
            P("tp", None),
            P("tp"),
            P(("sec", "dp"), None, "tp"),
            P("tp"),
            P(("sec", "dp"), "tp"),
            P(("sec", "dp"), None, "tp"),
        ),
        out_specs=(
            P(("sec", "dp"), None, "tp"),
            P(("sec", "dp"), None, "tp"),
            P(("sec", "dp"), None, "tp"),
            P(("sec", "dp"), "tp"),
        ),
        check_vma=False,
    )
```

```python
import jax
import jax.numpy as jnp
from jax import lax
from jax.experimental import pallas as pl
from jax.experimental.pallas import tpu as pltpu
from jax.sharding import PartitionSpec as P

WIDTH = 8192
MERGE_PATCHES = 4
PLANE = ("sec", "dp")
ALL = ("sec", "dp", "tp")
N_TP = 8
BF = jnp.bfloat16
F32 = jnp.float32


def plane_index(x, y, core):
    return (y % 2) * 16 + x * 4 + (y // 2) * 2 + core


SAME_CORE = [
    [plane_index(x, y, core) for lo in range(2) for x in range(4) for y in (lo, lo + 2)]
    for core in range(2)
]
SAME_X = [[plane_index(x, y, core) for y in range(4) for core in range(2)] for x in range(4)]
SAME_Y = [[plane_index(x, y, core) for x in range(4)] for y in range(4) for core in range(2)]


def swap_cores(block):
    return lax.ppermute(block, "dp", [(i, i ^ 1) for i in range(16)])


def swap_halves(block):
    return lax.ppermute(block, "sec", [(0, 1), (1, 0)])


def weight_to_plane():
    route = []
    for p in range(32):
        for t in range(N_TP):
            plane = p // 4
            route.append((p * N_TP + t, ((t ^ plane) * 4 + p % 4) * N_TP + plane))
    return route


def grad_from_plane():
    route = []
    for x in range(4):
        for y in range(4):
            for core in range(2):
                for t in range(N_TP):
                    source = plane_index(x, y, core) * N_TP + t
                    row = 4 * t + 2 * core + x // 2
                    route.append((source, row * N_TP + ((2 * y + x % 2) ^ t)))
    return route


def vision_kernel(left_ref, most_ref, rest_ref, bias_ref, out_ref):
    most = most_ref[:, 0].reshape(2048, 256)
    rest = rest_ref[:, 0].reshape(512, 256)
    total = jnp.dot(left_ref[:, :2048], most, preferred_element_type=F32)
    total += jnp.dot(left_ref[:, 2048:], rest, preferred_element_type=F32)
    out_ref[...] = (total + bias_ref[...]).astype(BF)


def vision_product(hidden, gathered, bias):
    rows, depth = hidden.shape
    return pl.pallas_call(
        vision_kernel,
        grid=(4,),
        in_specs=[
            pl.BlockSpec((rows, depth), lambda i: (0, 0)),
            pl.BlockSpec((8, 1, 256, 256), lambda i: (0, i, 1, 0)),
            pl.BlockSpec((8, 1, 64, 256), lambda i: (0, i, 8, 0)),
            pl.BlockSpec((1, 256), lambda i: (0, i)),
        ],
        out_specs=pl.BlockSpec((rows, 256), lambda i: (0, i)),
        out_shape=jax.ShapeDtypeStruct((rows, 1024), BF),
        cost_estimate=pl.CostEstimate(
            flops=2 * rows * depth * 1024, bytes_accessed=2 * depth * 1024, transcendentals=0
        ),
    )(hidden, gathered, gathered, bias[None])


def block_product_kernel(plane_ref, left_ref, right_ref, out_ref):
    out_ref[0] = jnp.dot(
        left_ref[...], right_ref[0].reshape(1024, 256), preferred_element_type=F32
    )


def block_product(left, gathered, plane):
    rows = left.shape[0]
    return pl.pallas_call(
        block_product_kernel,
        grid_spec=pltpu.PrefetchScalarGridSpec(
            num_scalar_prefetch=1,
            grid=(N_TP,),
            in_specs=[
                pl.BlockSpec((rows, 1024), lambda i, plane: (0, 0)),
                pl.BlockSpec((1, 4, 256, 256), lambda i, plane: (i, 0, 0, 0)),
            ],
            out_specs=pl.BlockSpec((1, rows, 256), lambda i, plane: (i ^ plane[0], 0, 0)),
        ),
        out_shape=jax.ShapeDtypeStruct((N_TP, rows, 256), F32),
        cost_estimate=pl.CostEstimate(
            flops=2 * rows * 1024 * 2048, bytes_accessed=4 << 20, transcendentals=0
        ),
    )(plane.astype(jnp.int32)[None], left, gathered)


def block_sum_kernel(left_ref, right_ref, out_ref):
    total = jnp.zeros(out_ref.shape, F32)
    for t in range(N_TP):
        total += lax.dot_general(
            left_ref[t],
            right_ref[t, 0],
            (((1,), (1,)), ((), ())),
            preferred_element_type=F32,
        )
    out_ref[...] = total


def block_sum(left, gathered):
    rows = left.shape[1]
    return pl.pallas_call(
        block_sum_kernel,
        grid=(4,),
        in_specs=[
            pl.BlockSpec((N_TP, rows, 256), lambda i: (0, 0, 0)),
            pl.BlockSpec((N_TP, 1, 256, 256), lambda i: (0, i, 0, 0)),
        ],
        out_specs=pl.BlockSpec((rows, 256), lambda i: (0, i)),
        out_shape=jax.ShapeDtypeStruct((rows, 1024), F32),
        cost_estimate=pl.CostEstimate(
            flops=2 * rows * 1024 * 2048, bytes_accessed=4 << 20, transcendentals=0
        ),
    )(left, gathered)


def line_product_kernel(normed_ref, cot_ref, out_ref):
    total = lax.dot_general(
        normed_ref[...].reshape(1024, 512),
        cot_ref[...].reshape(1024, 512),
        (((0,), (0,)), ((), ())),
        preferred_element_type=F32,
    )
    for i in range(4):
        row, col = i // 2 * 256, i % 2 * 256
        out_ref[i] = total[row : row + 256, col : col + 256].astype(BF)


def line_product(normed, cotangents):
    return pl.pallas_call(
        line_product_kernel,
        out_shape=jax.ShapeDtypeStruct((4, 256, 256), BF),
        cost_estimate=pl.CostEstimate(
            flops=2 * 1024 * 512 * 512, bytes_accessed=3 << 20, transcendentals=0
        ),
    )(normed, cotangents)


def flip_bits(blocks, number):
    shape = blocks.shape
    blocks = blocks.reshape((2, 2, 2) + shape[1:])
    for axis in range(3):
        bit = (number >> (2 - axis)) & 1
        blocks = jnp.where(bit == 1, jnp.flip(blocks, axis), blocks)
    return blocks.reshape(shape)


def layer_norm(values, gain_vector, bias_vector):
    average = jnp.mean(values, axis=-1, keepdims=True)
    centered = values - average
    variance = jnp.mean(centered * centered, axis=-1, keepdims=True)
    return centered * lax.rsqrt(variance + 1e-06) * gain_vector + bias_vector


def exchange_tp(blocks):
    return lax.all_to_all(blocks, "tp", 0, 0)


def gather_tp(block):
    return exchange_tp(jnp.broadcast_to(block[None], (N_TP,) + block.shape))


def per_device(
    patches,
    counts,
    positions,
    pe_weight,
    ln_gain,
    ln_bias,
    w_in,
    b_in,
    w_out,
    b_out,
    text_embeds,
    rms_gain,
    kv_weight,
    kv_cotangent,
):
    sec = lax.axis_index("sec")
    dp = lax.axis_index("dp")
    tp = lax.axis_index("tp")
    core = dp % 2
    image_count = counts[(1 - sec) * 16 + dp]

    tokens = patches.shape[1] // MERGE_PATCHES
    rows = patches[0].reshape(tokens, MERGE_PATCHES, -1).transpose(1, 0, 2)
    rows = jnp.pad(rows, ((0, 0), (0, 16 - tokens), (0, 0))).reshape(MERGE_PATCHES * 16, -1)
    patch_all = lax.all_gather(rows, "tp", tiled=True)

    place = sec * 16 + dp
    weight_block = lax.ppermute(kv_weight, ALL, weight_to_plane())
    share = lax.dynamic_slice_in_dim(w_out, place // 4 * 40, 40, axis=0)
    share = share.reshape(40, N_TP, 4, 256)
    share = lax.dynamic_index_in_dim(share, place % 4, axis=2, keepdims=False).transpose(1, 0, 2)
    share = exchange_tp(share).reshape(320, 256)

    columns, _ = lax.optimization_barrier((pe_weight.T, share))
    mine = lax.all_to_all(
        jnp.broadcast_to(columns[None], (16,) + columns.shape),
        PLANE,
        0,
        0,
        axis_index_groups=SAME_CORE,
    )
    shard = jnp.concatenate([weight_block, share], axis=0)
    gathered = lax.all_gather(shard, PLANE).reshape(8, 4, 576, 256)

    cot_input, mine = lax.optimization_barrier((kv_cotangent[0], mine))
    cotangents = gather_tp(cot_input)
    other = swap_cores(mine)
    first = jnp.where(core == 0, mine, other)
    second = jnp.where(core == 0, other, mine)
    full_patch = jnp.stack([first, second], axis=1).reshape(1280, -1)
    projected = lax.dot_general(
        patch_all, full_patch, (((1,), (1,)), ((), ())), preferred_element_type=F32
    )
    embedded = layer_norm(projected, ln_gain, ln_bias).astype(BF)
    embedded = embedded.reshape(N_TP, MERGE_PATCHES, 16, 1280)
    merged = jnp.concatenate(
        [embedded[:, m].reshape(N_TP * 16, 1280) for m in range(MERGE_PATCHES)], axis=1
    )
    before_gelu = jnp.dot(merged, w_in, preferred_element_type=F32) + b_in
    hidden = jax.nn.gelu(before_gelu, approximate=False).astype(BF)
    hidden = hidden.reshape(N_TP, 16, -1)[:, :tokens].reshape(N_TP * tokens, -1)
    hidden = swap_halves(hidden).T
    hidden, cotangents = lax.optimization_barrier((hidden, cotangents))
    hidden = gather_tp(hidden)

    cotangents = flip_bits(cotangents, tp)
    cot_line = cotangents
    cot_line = cot_line.reshape(4, 1, 2, 128, 256).transpose(0, 1, 3, 2, 4)
    cot_line = jnp.broadcast_to(cot_line, (4, 2, 128, 2, 256)).reshape(8, 128, 512)
    cot_line, hidden = lax.optimization_barrier((cot_line, hidden))
    cot_line = lax.all_to_all(cot_line, PLANE, 0, 0, axis_index_groups=SAME_X)

    hidden = hidden.reshape(N_TP, 8, 40, -1).transpose(1, 0, 2, 3).reshape(8, 320, -1)
    hidden = jnp.concatenate(
        [hidden[:, :256].reshape(2048, -1), hidden[:, 256:].reshape(512, -1)], axis=0
    ).T
    vision = vision_product(hidden, gathered, b_out)

    line_index = jnp.arange(128)
    slot_positions = positions[0]
    slot_ok = jnp.arange(112) < image_count
    selector = (slot_positions[None, :] == line_index[:, None]) & slot_ok[None, :]
    selector_bf = selector.astype(BF)
    placed = jnp.dot(selector_bf, vision, preferred_element_type=F32)
    image_rows = jnp.any(selector, axis=1, keepdims=True)
    combined = jnp.where(image_rows, placed, text_embeds[0].astype(F32))

    normed_grad = block_sum(cotangents, gathered)
    scaled = normed_grad * rms_gain
    stats = jnp.stack([jnp.sum(combined * combined, axis=1), jnp.sum(scaled * combined, axis=1)])
    stats, cot_line = lax.optimization_barrier((stats, cot_line))
    stats = jnp.sum(gather_tp(stats), axis=0)
    row_scale = lax.rsqrt(stats[0] / WIDTH + 1e-06)[:, None]
    row_dot = stats[1][:, None]

    gained = combined * rms_gain
    product = block_product(gained.astype(BF), gathered, tp)
    row_scale, product = lax.optimization_barrier((row_scale, product))
    normed = (gained * row_scale).astype(BF)
    normed = normed.reshape(128, 2, 512).transpose(1, 0, 2)
    normed_line = lax.all_to_all(
        jnp.broadcast_to(normed[None], (4, 2, 128, 512)).reshape(8, 128, 512),
        PLANE,
        0,
        0,
        axis_index_groups=SAME_X,
    )
    block = line_product(normed_line, cot_line)
    block = lax.all_to_all(block, PLANE, 0, 0, axis_index_groups=SAME_Y)
    block = jnp.sum(block.astype(F32), axis=0).astype(BF)
    kv_weight_grad = lax.ppermute(block, ALL, grad_from_plane()).astype(F32)

    keys_values = lax.psum_scatter(product, "tp", scatter_dimension=0, tiled=True)[0]
    keys_values = (keys_values * row_scale).astype(BF)

    seq_grad = (
        row_scale * scaled - combined * row_scale * row_scale * row_scale * row_dot / WIDTH
    ).astype(BF)
    image_grad = lax.dot_general(
        selector_bf, seq_grad, (((0,), (0,)), ((), ())), preferred_element_type=F32
    ).astype(BF)
    vision_grad = swap_halves(image_grad)
    return (keys_values[None], seq_grad[None], vision_grad[None], kv_weight_grad)


def solution(mesh):
    return jax.shard_map(
        per_device,
        mesh=mesh,
        in_specs=(
            P(("sec", "dp"), "tp", None),
            P(),
            P(("sec", "dp"), None),
            P(None, ("sec", "dp")),
            P(),
            P(),
            P(None, "tp"),
            P("tp"),
            P("tp", None),
            P("tp"),
            P(("sec", "dp"), None, "tp"),
            P("tp"),
            P(("sec", "dp"), "tp"),
            P(("sec", "dp"), None, "tp"),
        ),
        out_specs=(
            P(("sec", "dp"), None, "tp"),
            P(("sec", "dp"), None, "tp"),
            P(("sec", "dp"), None, "tp"),
            P(("sec", "dp"), "tp"),
        ),
        check_vma=False,
    )
```
